256 devices in a mesh: sx: 16 (over z, y_lo), sy: 16 (over y_hi, x, core).
Axes of the slice: x: 4, y: 4 (y_hi: 2, y_lo: 2; y = y_hi * 2 + y_lo), z: 8, core: 2. Of those that a mesh axis runs over, the one named last changes fastest.
Arguments:
- loads: bfloat16 [16, 16, 1024, 128], P('sx', 'sy'), may hold values from -6 to 6
- flex: float32 [16, 16, 1024, 1024], P('sx', 'sy'), may hold values from -1 to 9, as said below
- schur: bfloat16 [16, 16, 1024, 1024], P('sx', 'sy'), may hold values from -1 to 9, as said below
- couple: float32 [16, 16, 4, 1024], P('sx', 'sy'), may hold values from -3 to 3
- corner_perm: int32 [225], replicated, may hold values from 0 to 224, each once
- coarse_inverse: float32 [225, 225], replicated, may hold values from -1 to 4, as said below
Outputs:
- multipliers: float32 [16, 16, 2, 256, 128], P('sx', 'sy')
- residual: float32 [16, 16, 2, 256, 128], P('sx', 'sy')
The draws below stay inside these ranges and needn't reach their ends.
Inputs may be any that keep to these rules, and one draw needn't show every extreme that they name: `flex`: each subdomain's matrix is symmetric positive definite. `schur`: each subdomain's matrix is symmetric positive definite. `coarse_inverse`: symmetric positive definite.
All inputs are finite; a program needn't handle non-finite values.
Results may differ from the reference program's by a relative error of at most 0.009.
Values sent between devices are 32-bit elements; how exact they have to be, the bound alone decides.
A program may use at most 64 MiB of HBM per device.

```python
import math
import jax
import jax.numpy as jnp
from jax import lax

EDGE = 256
IFACE = 1024
LOADS = 128
ITERS = 4
NC = 225
N_SX = 16
N_SY = 16


def symmetric_noise(key, shape):
    noise = jax.random.truncated_normal(key, -4.0, 4.0, shape, jnp.float32)
    return 0.5 * (noise + jnp.swapaxes(noise, -1, -2))


def interface_matrix(key, lowest, highest):
    key_noise, key_scale = jax.random.split(key)
    scales = jnp.exp(jax.random.uniform(key_scale, (N_SX, N_SY, IFACE), jnp.float32, math.log(lowest), math.log(highest)))
    noise = symmetric_noise(key_noise, (N_SX, N_SY, IFACE, IFACE))
    inner_mat = jnp.eye(IFACE, dtype=jnp.float32) + 0.6 / math.sqrt(2.0 * IFACE) * noise
    return scales[..., :, None] * inner_mat * scales[..., None, :]


def draw_flex(key, part):
    return interface_matrix(jax.random.fold_in(key, 11), 0.5, 2.0)


def draw_schur(key, part):
    return interface_matrix(jax.random.fold_in(key, 23), 0.5, 2.0).astype(jnp.bfloat16)


def rising_factor(rise):
    position = jnp.arange(N_SX * N_SY, dtype=jnp.float32).reshape(N_SX, N_SY) / (N_SX * N_SY - 1.0)
    return (1.0 + rise * position)[:, :, None, None]


def draw_couple(key, part):
    key = jax.random.fold_in(key, 41)
    base = 0.3 * float(IFACE) ** (-0.25)
    noise = jax.random.truncated_normal(key, -4.0, 4.0, (N_SX, N_SY, 4, IFACE), jnp.float32)
    return base * rising_factor(2.0) * noise


def draw_coarse_inverse(key, part):
    key_noise, key_diag = jax.random.split(jax.random.fold_in(key, 37))
    diagonal = jnp.exp(jax.random.uniform(key_diag, (NC,), jnp.float32, math.log(1.5), math.log(3.0)))
    noise = symmetric_noise(key_noise, (NC, NC))
    return jnp.eye(NC, dtype=jnp.float32) * diagonal[:, None] + 0.7 / math.sqrt(1.0 * NC) * noise


def shard_levels(stream_key, extent, cuts, low, high):
    level = 1.0
    for axis_at, shards_of in cuts:
        steps = jax.random.uniform(jax.random.fold_in(jax.random.fold_in(stream_key, 6), axis_at), (shards_of,), jnp.float32, low / len(cuts), high / len(cuts))
        level = level * jnp.repeat(jnp.exp(steps), extent[axis_at] // shards_of).reshape((-1,) + (1,) * (len(extent) - 1 - axis_at))
    return level


def bell_draw(own_key, shape, scale, reach, cuts=(), held_as=jnp.bfloat16):
    values = scale * jax.random.normal(own_key, shape, jnp.float32)
    if cuts:
        values = values * shard_levels(own_key, shape, cuts, -0.22, 0.18)
    return jnp.clip(values, -reach, reach).astype(held_as)


def setup_inputs(seed: int = 0) -> dict:
    streams_of = jax.random.split(jax.random.key(seed), 7)
    loads = bell_draw(streams_of[0], (N_SX, N_SY, IFACE, LOADS), 1.0, 6.0, ((0, 16), (1, 16)))
    flex = draw_flex(jax.random.fold_in(streams_of[6], 71), 0)
    schur = draw_schur(jax.random.fold_in(streams_of[6], 71), 0)
    couple = draw_couple(jax.random.fold_in(streams_of[6], 71), 0)
    corner_perm = jax.random.permutation(streams_of[4], NC).astype(jnp.int32)
    coarse_inverse = draw_coarse_inverse(jax.random.fold_in(streams_of[6], 71), 0)
    return {"loads": loads, "flex": flex, "schur": schur, "couple": couple, "corner_perm": corner_perm, "coarse_inverse": coarse_inverse}


def corner_numbers(corner_perm):
    grid_row = jnp.arange(N_SX, dtype=jnp.int32)[:, None, None] + jnp.arange(4, dtype=jnp.int32)[None, None, :] // 2
    grid_col = jnp.arange(N_SY, dtype=jnp.int32)[None, :, None] + jnp.arange(4, dtype=jnp.int32)[None, None, :] % 2
    inside = (grid_row >= 1) & (grid_row <= N_SX - 1) & (grid_col >= 1) & (grid_col <= N_SY - 1)
    structural = jnp.clip((grid_row - 1) * (N_SY - 1) + grid_col - 1, 0, NC - 1).astype(jnp.int32)
    return jnp.where(inside, corner_perm[structural], NC).astype(jnp.int32)


def spread(dual_vec):
    vertical = dual_vec[:, :, 0]
    horizontal = dual_vec[:, :, 1]
    above = jnp.concatenate([jnp.zeros_like(vertical[:1]), vertical[:-1]], 0)
    beside = jnp.concatenate([jnp.zeros_like(horizontal[:, :1]), horizontal[:, :-1]], 1)
    return jnp.concatenate([-above, vertical, -beside, horizontal], 2)


def jump(local_vec):
    upper = local_vec[:, :, :EDGE]
    lower = local_vec[:, :, EDGE:2 * EDGE]
    west = local_vec[:, :, 2 * EDGE:3 * EDGE]
    east = local_vec[:, :, 3 * EDGE:]
    below = jnp.concatenate([upper[1:], jnp.zeros_like(upper[:1])], 0)
    right = jnp.concatenate([west[:, 1:], jnp.zeros_like(west[:, :1])], 1)
    keep_vertical = (jnp.arange(N_SX) < N_SX - 1).astype(jnp.float32)[:, None, None, None]
    keep_horizontal = (jnp.arange(N_SY) < N_SY - 1).astype(jnp.float32)[None, :, None, None]
    return jnp.stack([(lower - below) * keep_vertical, (east - right) * keep_horizontal], 2)


def batched_products(matrices, vectors):
    flat_mats = matrices.reshape(N_SX * N_SY, IFACE, IFACE)
    flat_vecs = vectors.reshape(N_SX * N_SY, IFACE, LOADS)

    def single(pair):
        return jnp.dot(pair[0], pair[1], preferred_element_type=jnp.float32)

    return lax.map(single, (flat_mats, flat_vecs)).reshape(N_SX, N_SY, IFACE, LOADS)


def precise_products(matrices, vectors):
    flat_mats = matrices.reshape(N_SX * N_SY, IFACE, IFACE)
    flat_vecs = vectors.reshape(N_SX * N_SY, IFACE, LOADS)

    def single(pair):
        return jnp.dot(pair[0], pair[1], precision=lax.Precision.HIGHEST)

    return lax.map(single, (flat_mats, flat_vecs)).reshape(N_SX, N_SY, IFACE, LOADS)


def operator_local(vec_f32, flex, couple, numbers, coarse_inverse):
    highest = lax.Precision.HIGHEST
    partial_value = jnp.einsum("xykm,xymr->xykr", couple, vec_f32, precision=highest)
    summed = jax.ops.segment_sum(partial_value.reshape(-1, LOADS), numbers.reshape(-1), num_segments=NC + 1)[:NC]
    solved = jnp.dot(coarse_inverse, summed, precision=highest)
    padded = jnp.concatenate([solved, jnp.zeros((1, LOADS), solved.dtype)], 0)
    picked = padded[numbers]
    return precise_products(flex, vec_f32) + jnp.einsum("xykm,xykr->xymr", couple, picked, precision=highest)


def reference(loads, flex, schur, couple, corner_perm, coarse_inverse):
    numbers = corner_numbers(corner_perm)

    def apply_dual(dual_vec):
        return jump(operator_local(spread(dual_vec), flex, couple, numbers, coarse_inverse))

    def precondition(dual_vec):
        halved = (0.5 * spread(dual_vec)).astype(jnp.bfloat16)
        return 0.5 * jump(batched_products(schur, halved))

    def inner(first, second):
        return jnp.sum(first * second, axis=(0, 1, 2, 3))

    gap = jump(operator_local(loads.astype(jnp.float32), flex, couple, numbers, coarse_inverse))
    multipliers = jnp.zeros_like(gap)
    residual = gap
    pre_vec = precondition(residual)
    direction = pre_vec
    rz_now = inner(residual, pre_vec)
    for step_index in range(ITERS):
        image = apply_dual(direction)
        step_size = rz_now / inner(direction, image)
        multipliers = multipliers + step_size * direction
        residual = residual - step_size * image
        if step_index < ITERS - 1:
            pre_vec = precondition(residual)
            rz_next = inner(residual, pre_vec)
            direction = pre_vec + (rz_next / rz_now) * direction
            rz_now = rz_next
    return multipliers, residual
```

```python
import functools

import jax
import jax.numpy as jnp
from jax import lax
from jax.experimental import pallas as pl
from jax.experimental.pallas import tpu as pltpu
from jax.sharding import PartitionSpec as P

ITERS = 4
MESH = pl.DeviceIdType.MESH
F32 = jnp.float32
BF16 = jnp.bfloat16
OPPOSITE = (1, 0, 3, 2)
NEAR = ((-1, 0), (1, 0), (0, -1), (0, 1))


def dot(a, b):
    return jnp.dot(a, b, preferred_element_type=F32)


def halves(x):
    high = x.astype(BF16)
    return high, (x - high.astype(F32)).astype(BF16)


def dot3(a_high, a_low, b_high, b_low):
    return dot(a_high, b_high) + (dot(a_high, b_low) + dot(a_low, b_high))


def colsum(x):
    return jnp.sum(x, axis=0, keepdims=True)


def iota(shape, dim):
    return lax.broadcasted_iota(jnp.int32, shape, dim)


def kernel(
    nx, ny, edge, group,
    loads_ref, flex_hbm, schur_hbm, couple_ref, perm_ref, cinv_ref,
    mult_ref, resid_ref,
    flex_v, flex_hi, flex_lo, schur_v, cpad, ck_hi, ck_lo, solve_hi, solve_lo,
    pick, cpl_hi, cpl_lo, cown, cnear, bt,
    recv, send, own_a, own_b, first, own_c, second,
    u_ref, u_hi, u_lo, r_ref, s_ref, p_ref,
    flex_sem, schur_sem, cs_sem, cr_sem, ex_send, ex_recv, f_send, f_recv, g_send, g_recv,
):
    i = lax.axis_index("sx")
    j = lax.axis_index("sy")
    exists = (i > 0, i < nx - 1, j > 0, j < ny - 1)
    near = tuple((i + di, j + dj) for di, dj in NEAR)
    kdim = ny * group

    def rows(e):
        return pl.ds(e * edge, edge)

    def flex_copy(e):
        return pltpu.make_async_copy(flex_hbm.at[rows(e)], flex_v.at[rows(e)], flex_sem.at[e])

    for e in range(4):
        flex_copy(e).start()
    schur_copy = pltpu.make_async_copy(schur_hbm, schur_v, schur_sem)
    schur_copy.start()

    barrier = pltpu.get_barrier_semaphore()

    @pl.loop(1, nx)
    def _(d):
        pl.semaphore_signal(barrier, inc=1, device_id=(lax.rem(i + d, nx), j), device_id_type=MESH)

    @pl.when(j < ny - 1)
    def _():
        @pl.loop(0, nx)
        def _(d):
            pl.semaphore_signal(barrier, inc=1, device_id=(d, j + 1), device_id_type=MESH)

    @pl.loop(0, ny)
    def _(d):
        @pl.when((d != j) & (d != j + 1))
        def _():
            pl.semaphore_signal(barrier, inc=1, device_id=(i, d), device_id_type=MESH)

    nc = cinv_ref.shape[0]
    cpad[...] = jnp.zeros_like(cpad)
    cpad[0:nc, 0:nc] = cinv_ref[...]
    order = jnp.where(iota((cpad.shape[0], kdim), 0) == perm_ref[...], 1.0, 0.0).astype(BF16)
    m_rows = solve_hi.shape[0]
    m_id = iota((m_rows, kdim), 0)
    col = iota((m_rows, kdim), 1)
    corner_p = i - 1 + (m_id >> 2)
    corner_q = j - 1 + (m_id & 3)
    inside = (m_id < 16) & (corner_p >= 1) & (corner_p <= nx - 1) & (corner_q >= 1) & (corner_q <= ny - 1)
    wanted = group * (corner_q - 1) + corner_p - 1
    select = jnp.where(inside & (col == wanted), 1.0, 0.0).astype(BF16)
    col_in = col - group * ((col * (65536 // group + 1)) >> 16)
    totals = jnp.where((m_id >= 16) & (col_in == m_id - 16 + group - 8), 1.0, 0.0)
    c_high, c_low = halves(cpad[...])
    contract0 = (((0,), (0,)), ((), ()))
    for part, out, solve in ((c_high, ck_hi, solve_hi), (c_low, ck_lo, solve_lo)):
        right = dot(part, order).astype(BF16)
        out[...] = lax.dot_general(order, right, contract0, preferred_element_type=F32).astype(BF16)
        solve[...] = (dot(select, out[...]) + (totals if out is ck_hi else 0.0)).astype(BF16)

    pm = iota(pick.shape, 0)
    pn = iota(pick.shape, 1)
    slot = pn >> 3
    row = pn & 7
    source = slot - jnp.where(slot >= nx, nx, 0)
    corner_row = (pm < nx - 1) & (row < 2) & (source + row == pm + 1)
    scalar_row = (pm >= group - 8) & (slot < nx) & (row >= 2) & (row - 2 == pm - (group - 8))
    pick[...] = jnp.where(corner_row | scalar_row, 1.0, 0.0).astype(BF16)

    couple_all = couple_ref[...]
    zero6 = jnp.zeros((6, couple_all.shape[1]), F32)
    stacked = jnp.concatenate(
        [couple_all[1:2], couple_all[3:4], zero6, couple_all[0:1], couple_all[2:3], zero6], 0
    )
    cpl_hi[...], cpl_lo[...] = halves(stacked)
    for e in range(4):
        cown[e] = jnp.concatenate(
            [couple_all[:, e * edge : (e + 1) * edge], jnp.zeros((4, edge), F32)], 0
        )
    s_ref[...] = jnp.zeros_like(s_ref)
    p_ref[...] = jnp.zeros_like(p_ref)
    mult_ref[...] = jnp.zeros_like(mult_ref)

    @pl.when(j == ny - 1)
    def _():
        first[:, nx:, :, :] = jnp.zeros((ITERS + 1, nx, 8, first.shape[-1]), F32)

    sends_to = (nx - 1) + (ny - 1)

    @pl.when(j > 0)
    def _():
        pl.semaphore_wait(barrier, sends_to + nx - 1)

    @pl.when(j == 0)
    def _():
        pl.semaphore_wait(barrier, sends_to)

    def couple_copy(e):
        return pltpu.make_async_remote_copy(
            src_ref=cown.at[e], dst_ref=cnear.at[OPPOSITE[e]],
            send_sem=cs_sem.at[e], recv_sem=cr_sem.at[OPPOSITE[e]],
            device_id=near[e], device_id_type=MESH,
        )

    def couple_arrival(e):
        return pltpu.make_async_remote_copy(
            src_ref=cown.at[e], dst_ref=cnear.at[e],
            send_sem=cs_sem.at[e], recv_sem=cr_sem.at[e],
            device_id=near[e], device_id_type=MESH,
        )

    for e in range(4):
        pl.when(exists[e])(lambda e=e: couple_copy(e).start())

    def edge_copy(t, e):
        return pltpu.make_async_remote_copy(
            src_ref=send.at[t, e], dst_ref=recv.at[t, OPPOSITE[e]],
            send_sem=ex_send.at[t, e], recv_sem=ex_recv.at[t, OPPOSITE[e]],
            device_id=near[e], device_id_type=MESH,
        )

    def edge_arrival(t, e):
        return pltpu.make_async_remote_copy(
            src_ref=send.at[t, e], dst_ref=recv.at[t, e],
            send_sem=ex_send.at[t, e], recv_sem=ex_recv.at[t, e],
            device_id=near[e], device_id_type=MESH,
        )

    def corner_partials(with_low):
        if with_low:
            return dot3(cpl_hi[...], cpl_lo[...], u_hi[...], u_lo[...])
        return dot(cpl_hi[...], u_hi[...]) + dot(cpl_lo[...], u_hi[...])

    def first_stage(k, partial, scalars):
        row_id = iota((8, partial.shape[1]), 0)
        message = partial[0:8]
        for n, value in enumerate(scalars):
            message = jnp.where(row_id == n + 2, value, message)
        own_a[k] = message
        own_b[k] = partial[8:16]
        first[k, i] = message

        @pl.loop(1, nx)
        def _(d):
            pltpu.make_async_remote_copy(
                src_ref=own_a.at[k], dst_ref=first.at[k, i],
                send_sem=f_send.at[k], recv_sem=f_recv.at[k],
                device_id=(lax.rem(i + d, nx), j), device_id_type=MESH,
            ).start()

        @pl.when(j > 0)
        def _():
            @pl.loop(0, nx)
            def _(d):
                pltpu.make_async_remote_copy(
                    src_ref=own_b.at[k], dst_ref=first.at[k, nx + i],
                    send_sem=f_send.at[k], recv_sem=f_recv.at[k],
                    device_id=(lax.rem(i + d, nx), j - 1), device_id_type=MESH,
                ).start()

    def bytes_of(ref, sem):
        return pltpu.make_async_copy(ref, ref, sem)

    def second_stage(k):
        @pl.when(j < ny - 1)
        def _():
            bytes_of(first.at[k, pl.ds(0, 2 * nx - 1)], f_recv.at[k]).wait()

        @pl.when(j == ny - 1)
        def _():
            bytes_of(first.at[k, pl.ds(0, nx - 1)], f_recv.at[k]).wait()

        got_high, got_low = halves(first[k].reshape(2 * nx * 8, first.shape[-1]))
        summed = dot(pick[...], got_high) + dot(pick[...], got_low)
        own_c[k] = summed
        second[k, j] = summed

        @pl.loop(1, ny)
        def _(d):
            pltpu.make_async_remote_copy(
                src_ref=own_c.at[k], dst_ref=second.at[k, j],
                send_sem=g_send.at[k], recv_sem=g_recv.at[k],
                device_id=(i, lax.rem(j + d, ny)), device_id_type=MESH,
            ).start()

    def coarse_solve(k, with_energy):
        bytes_of(second.at[k, pl.ds(0, ny - 1)], g_recv.at[k]).wait()
        gathered = second[k].reshape(kdim, second.shape[-1])
        g_high, g_low = halves(gathered)
        local = dot3(solve_hi[...], solve_lo[...], g_high, g_low)
        z_high, z_low = halves(local[0:16])
        z_stack = jnp.concatenate([z_high, z_low, z_high], 0)
        energy = None
        if with_energy:
            energy = colsum(gathered * dot3(ck_hi[...], ck_lo[...], g_high, g_low))
        return z_stack, local[16:24], energy

    def flex_products(k, e_list, last):
        energy = 0.0
        for e in e_list:
            product = dot(flex_hi[rows(e)], u_hi[...]) + dot(flex_lo[rows(e)], u_hi[...])
            send[k, e] = product
            if e in (0, 2):
                pl.when(exists[e])(lambda e=e: edge_copy(k, e).start())
            else:
                pl.when(exists[e] & jnp.logical_not(last))(lambda e=e: edge_copy(k, e).start())
            energy = energy + colsum(u_ref[e] * product)
        return energy

    loads = loads_ref[...]
    u_hi[...] = loads
    for e in range(4):
        u_ref[e] = loads[e * edge : (e + 1) * edge].astype(F32)
    zero_row = jnp.zeros((1, loads.shape[1]), F32)
    first_stage(0, corner_partials(False), (zero_row, zero_row, zero_row))
    for e in range(4):
        flex_copy(e).wait()
        flex_hi[rows(e)], flex_lo[rows(e)] = halves(flex_v[rows(e)])
        flex_products(0, (e,), False)
    schur_copy.wait()
    second_stage(0)

    for e in range(4):
        bt[rows(e)] = jnp.zeros((edge, 48), BF16)

        def build(e=e):
            couple_arrival(e).wait_recv()
            kk = iota((8, 48), 0)
            corner = iota((8, 48), 1) & 15

            def placed(dp, dq):
                at = 4 * (dp + (kk >> 1)) + dq + (kk & 1)
                return jnp.where((corner == at) & (kk < 4), 1.0, 0.0)

            di, dj = NEAR[e]
            highest = lax.Precision.HIGHEST
            mixed = jnp.dot(cown[e].T, placed(1, 1), precision=highest) - jnp.dot(
                cnear[e].T, placed(1 + di, 1 + dj), precision=highest
            )
            high, low = halves(mixed)
            bt[rows(e)] = jnp.where(
                iota(mixed.shape, 1) < 32, high.astype(F32), low.astype(F32)
            ).astype(BF16)

        pl.when(exists[e])(build)

    z_stack, _, _ = coarse_solve(0, False)
    for e in range(4):
        r_ref[e] = jnp.zeros(r_ref.shape[1:], F32)

        def arrived(e=e):
            edge_arrival(0, e).wait_recv()
            r_ref[e] = send[0, e] - recv[0, e] + dot(bt[rows(e)], z_stack)

        pl.when(exists[e])(arrived)

    def iteration(k, carry):
        rz_old, energy_old = carry
        last = k == ITERS
        t = ITERS + k
        for e in range(4):
            u_hi[rows(e)] = (0.5 * r_ref[e]).astype(BF16)
        for e in range(4):
            send[t, e] = 0.5 * dot(schur_v[rows(e)], u_hi[...])
            pl.when(exists[e])(lambda e=e: edge_copy(t, e).start())
        for e in range(4):
            u_ref[e] = jnp.zeros(u_ref.shape[1:], F32)

            def arrived(e=e):
                edge_arrival(t, e).wait_recv()
                u_ref[e] = send[t, e] - recv[t, e]

            pl.when(exists[e])(arrived)
            u_hi[rows(e)], u_lo[rows(e)] = halves(u_ref[e])
        rz_part = 0.5 * sum(colsum(r_ref[e] * u_ref[e]) for e in range(4))
        cross_part = 0.5 * sum(colsum(s_ref[e] * u_ref[e]) for e in range(4))
        partial = corner_partials(True)
        flex_part = flex_products(k, range(4), last)
        first_stage(k, partial, (rz_part, cross_part, flex_part))
        second_stage(k)
        z_stack, totals, coarse_part = coarse_solve(k, True)
        rz = totals[0:1]
        cross = totals[1:2]
        beta = jnp.where(k == 1, 0.0, rz / rz_old)
        energy = totals[2:3] + coarse_part + beta * (2.0 * cross + beta * energy_old)
        step = rz / energy
        for n, e in enumerate((1, 3)):
            direction = u_ref[e] + beta * p_ref[n]
            p_ref[n] = direction
            mult_ref[n] = mult_ref[n] + step * direction
        for e in range(4):

            def arrived(e=e):
                edge_arrival(k, e).wait_recv()
                image = send[k, e] - recv[k, e] + dot(bt[rows(e)], z_stack)
                image = image + beta * s_ref[e]
                s_ref[e] = image
                r_ref[e] = r_ref[e] - step * image

            if e in (1, 3):
                pl.when(exists[e])(arrived)
            else:
                pl.when(exists[e] & jnp.logical_not(last))(arrived)
        return rz, energy

    lax.fori_loop(1, ITERS + 1, iteration, (zero_row + 1.0, zero_row))
    resid_ref[0] = r_ref[1]
    resid_ref[1] = r_ref[3]

    for e in range(4):
        pl.when(exists[e])(lambda e=e: couple_copy(e).wait_send())

    @pl.loop(0, 2 * ITERS + 1)
    def _(t):
        for e in range(4):
            if e in (0, 2):
                pl.when(exists[e])(lambda e=e: edge_copy(t, e).wait_send())
            else:
                pl.when(exists[e] & (t != ITERS))(lambda e=e: edge_copy(t, e).wait_send())

    @pl.loop(0, ITERS + 1)
    def _(k):
        @pl.when(j > 0)
        def _():
            bytes_of(first.at[k, pl.ds(0, 2 * nx - 1)], f_send.at[k]).wait()

        @pl.when(j == 0)
        def _():
            bytes_of(first.at[k, pl.ds(0, nx - 1)], f_send.at[k]).wait()

        bytes_of(second.at[k, pl.ds(0, ny - 1)], g_send.at[k]).wait()


def per_device(loads, flex, schur, couple, corner_perm, coarse_inverse):
    nx = lax.axis_size("sx")
    ny = lax.axis_size("sy")
    iface, cols = loads.shape[2:]
    edge = iface // 4
    nc = coarse_inverse.shape[0]
    ncp = -(-nc // 128) * 128
    group = -(-(nx - 1) // 8) * 8 + 8
    kdim = ny * group
    perm = corner_perm.reshape(nx - 1, ny - 1).T
    perm = jnp.pad(perm, ((0, 1), (0, group - (nx - 1))), constant_values=-1).reshape(1, kdim)
    steps = 2 * ITERS + 1
    rounds = ITERS + 1
    vmem = pl.BlockSpec(memory_space=pltpu.VMEM)
    hbm = pl.BlockSpec(memory_space=pl.ANY)
    dma = pltpu.SemaphoreType.DMA
    out = jax.ShapeDtypeStruct((2, edge, cols), F32)
    mult, resid = pl.pallas_call(
        functools.partial(kernel, nx, ny, edge, group),
        out_shape=(out, out),
        in_specs=[vmem, hbm, hbm, vmem, vmem, vmem],
        out_specs=(vmem, vmem),
        scratch_shapes=[
            pltpu.VMEM((iface, iface), F32),
            pltpu.VMEM((iface, iface), BF16),
            pltpu.VMEM((iface, iface), BF16),
            pltpu.VMEM((iface, iface), BF16),
            pltpu.VMEM((ncp, ncp), F32),
            pltpu.VMEM((kdim, kdim), BF16),
            pltpu.VMEM((kdim, kdim), BF16),
            pltpu.VMEM((24, kdim), BF16),
            pltpu.VMEM((24, kdim), BF16),
            pltpu.VMEM((group, 2 * nx * 8), BF16),
            pltpu.VMEM((16, iface), BF16),
            pltpu.VMEM((16, iface), BF16),
            pltpu.VMEM((4, 8, edge), F32),
            pltpu.VMEM((4, 8, edge), F32),
            pltpu.VMEM((iface, 48), BF16),
            pltpu.VMEM((steps, 4, edge, cols), F32),
            pltpu.VMEM((steps, 4, edge, cols), F32),
            pltpu.VMEM((rounds, 8, cols), F32),
            pltpu.VMEM((rounds, 8, cols), F32),
            pltpu.VMEM((rounds, 2 * nx, 8, cols), F32),
            pltpu.VMEM((rounds, group, cols), F32),
            pltpu.VMEM((rounds, ny, group, cols), F32),
            pltpu.VMEM((4, edge, cols), F32),
            pltpu.VMEM((iface, cols), BF16),
            pltpu.VMEM((iface, cols), BF16),
            pltpu.VMEM((4, edge, cols), F32),
            pltpu.VMEM((4, edge, cols), F32),
            pltpu.VMEM((2, edge, cols), F32),
            dma((4,)),
            dma,
            dma((4,)),
            dma((4,)),
            dma((steps, 4)),
            dma((steps, 4)),
            dma((rounds,)),
            dma((rounds,)),
            dma((rounds,)),
            dma((rounds,)),
        ],
        compiler_params=pltpu.CompilerParams(
            collective_id=0, has_side_effects=True, vmem_limit_bytes=48 * 1024 * 1024
        ),
    )(loads[0, 0], flex[0, 0], schur[0, 0], couple[0, 0], perm, coarse_inverse)
    return mult[None, None], resid[None, None]


def solution(mesh):
    placed = (
        P("sx", "sy", None, None),
        P("sx", "sy", None, None),
        P("sx", "sy", None, None),
        P("sx", "sy", None, None),
        P(),
        P(),
    )
    return jax.shard_map(
        per_device,
        mesh=mesh,
        in_specs=placed,
        out_specs=(P("sx", "sy", None, None, None), P("sx", "sy", None, None, None)),
        check_vma=False,
    )
```

```python
import functools

import jax
import jax.numpy as jnp
from jax import lax
from jax.experimental import pallas as pl
from jax.experimental.pallas import tpu as pltpu
from jax.sharding import PartitionSpec as P

ITERS = 4
ZROWS = 48
MESH = pl.DeviceIdType.MESH
F32 = jnp.float32
BF16 = jnp.bfloat16
OPPOSITE = (1, 0, 3, 2)
NEAR = ((-1, 0), (1, 0), (0, -1), (0, 1))


def dot(a, b):
    return jnp.dot(a, b, preferred_element_type=F32)


def halves(x):
    high = x.astype(BF16)
    return high, (x - high.astype(F32)).astype(BF16)


def dot3(a_high, a_low, b_high, b_low):
    return dot(a_high, b_high) + (dot(a_high, b_low) + dot(a_low, b_high))


def colsum(x):
    return jnp.sum(x, axis=0, keepdims=True)


def iota(shape, dim):
    return lax.broadcasted_iota(jnp.int32, shape, dim)


def kernel(
    nx, ny, edge, group,
    loads_ref, flex_hbm, schur_hbm, couple_ref, perm_ref, cinv_ref,
    mult_ref, resid_ref,
    flex_v, flex_2, schur_v, cpad, ck_2, solve_2,
    pick, cpl_2, cown, cnear, b_rows, bt, g_rows, g_near, mbt,
    recv, send, own_a, own_b, first, own_c, second,
    u_ref, weights, z_ref, r_ref, s_ref, q_ref, p_ref,
    flex_sem, schur_sem, cs_sem, cr_sem, gs_sem, gr_sem,
    ex_send, ex_recv, f_send, f_recv, g_send, g_recv,
):
    i = lax.axis_index("sx")
    j = lax.axis_index("sy")
    exists = (i > 0, i < nx - 1, j > 0, j < ny - 1)
    near = tuple((i + di, j + dj) for di, dj in NEAR)
    kdim = ny * group
    cols = loads_ref.shape[1]
    highest = lax.Precision.HIGHEST

    def rows(e):
        return pl.ds(e * edge, edge)

    def flex_copy(e):
        return pltpu.make_async_copy(flex_hbm.at[rows(e)], flex_v.at[rows(e)], flex_sem.at[e])

    for e in range(4):
        flex_copy(e).start()
    schur_copy = pltpu.make_async_copy(schur_hbm, schur_v, schur_sem)
    schur_copy.start()

    barrier = pltpu.get_barrier_semaphore()

    @pl.loop(1, nx)
    def _(d):
        pl.semaphore_signal(barrier, inc=1, device_id=(lax.rem(i + d, nx), j), device_id_type=MESH)

    @pl.when(j < ny - 1)
    def _():
        @pl.loop(0, nx)
        def _(d):
            pl.semaphore_signal(barrier, inc=1, device_id=(d, j + 1), device_id_type=MESH)

    @pl.loop(0, ny)
    def _(d):
        @pl.when((d != j) & (d != j + 1))
        def _():
            pl.semaphore_signal(barrier, inc=1, device_id=(i, d), device_id_type=MESH)

    couple_all = couple_ref[...]
    zero6 = jnp.zeros((6, couple_all.shape[1]), F32)
    stacked = jnp.concatenate(
        [couple_all[1:2], couple_all[3:4], zero6, couple_all[0:1], couple_all[2:3], zero6], 0
    )
    cpl_2[0:16], cpl_2[16:32] = halves(stacked)
    for e in range(4):
        cown[e] = jnp.concatenate(
            [couple_all[:, e * edge : (e + 1) * edge], jnp.zeros((4, edge), F32)], 0
        )

    pm = iota(pick.shape, 0)
    pn = iota(pick.shape, 1)
    slot = pn >> 3
    row = pn & 7
    source = slot - jnp.where(slot >= nx, nx, 0)
    corner_row = (pm < nx - 1) & (row < 2) & (source + row == pm + 1)
    scalar_row = (pm >= group - 8) & (slot < nx) & (row >= 2) & (row - 2 == pm - (group - 8))
    pick[...] = jnp.where(corner_row | scalar_row, 1.0, 0.0).astype(BF16)

    for ref in (r_ref, s_ref, q_ref, p_ref, mult_ref, u_ref):
        ref[...] = jnp.zeros_like(ref)

    @pl.when(j == ny - 1)
    def _():
        first[:, nx:, :, :] = jnp.zeros((ITERS + 1, nx, 8, cols), F32)

    def coarse_operator():
        nc = cinv_ref.shape[0]
        cpad[...] = jnp.zeros_like(cpad)
        cpad[0:nc, 0:nc] = cinv_ref[...]
        order = jnp.where(iota((cpad.shape[0], kdim), 0) == perm_ref[...], 1.0, 0.0).astype(BF16)
        m_id = iota((ZROWS + 8, kdim), 0)
        col = iota((ZROWS + 8, kdim), 1)
        block_row = (m_id * 43) >> 8
        corner_p = i - 2 + block_row
        corner_q = j - 2 + m_id - 6 * block_row
        inside = (m_id < 36) & (corner_p >= 1) & (corner_p <= nx - 1)
        inside = inside & (corner_q >= 1) & (corner_q <= ny - 1)
        wanted = group * (corner_q - 1) + corner_p - 1
        select = jnp.where(inside & (col == wanted), 1.0, 0.0).astype(BF16)
        col_in = col - group * ((col * (65536 // group + 1)) >> 16)
        totals = jnp.where((m_id >= ZROWS) & (col_in == m_id - ZROWS + group - 8), 1.0, 0.0)
        contract0 = (((0,), (0,)), ((), ()))
        for n, part in enumerate(halves(cpad[...])):
            right = dot(part, order).astype(BF16)
            full = lax.dot_general(order, right, contract0, preferred_element_type=F32).astype(BF16)
            ck_2[n] = full
            solve_2[n] = (dot(select, full) + (totals if n == 0 else 0.0)).astype(BF16)

    def couple_copy(e):
        return pltpu.make_async_remote_copy(
            src_ref=cown.at[e], dst_ref=cnear.at[OPPOSITE[e]],
            send_sem=cs_sem.at[e], recv_sem=cr_sem.at[OPPOSITE[e]],
            device_id=near[e], device_id_type=MESH,
        )

    def couple_arrival(e):
        return pltpu.make_async_remote_copy(
            src_ref=cown.at[e], dst_ref=cnear.at[e],
            send_sem=cs_sem.at[e], recv_sem=cr_sem.at[e],
            device_id=near[e], device_id_type=MESH,
        )

    def image_copy(e):
        return pltpu.make_async_remote_copy(
            src_ref=g_rows.at[e, pl.ds(0, 32)], dst_ref=g_near.at[OPPOSITE[e], pl.ds(0, 32)],
            send_sem=gs_sem.at[e], recv_sem=gr_sem.at[OPPOSITE[e]],
            device_id=near[e], device_id_type=MESH,
        )

    def image_arrival(e):
        return pltpu.make_async_remote_copy(
            src_ref=g_rows.at[e, pl.ds(0, 32)], dst_ref=g_near.at[e, pl.ds(0, 32)],
            send_sem=gs_sem.at[e], recv_sem=gr_sem.at[e],
            device_id=near[e], device_id_type=MESH,
        )

    def edge_copy(t, e):
        return pltpu.make_async_remote_copy(
            src_ref=send.at[t, e], dst_ref=recv.at[t, OPPOSITE[e]],
            send_sem=ex_send.at[t, e], recv_sem=ex_recv.at[t, OPPOSITE[e]],
            device_id=near[e], device_id_type=MESH,
        )

    def edge_arrival(t, e):
        return pltpu.make_async_remote_copy(
            src_ref=send.at[t, e], dst_ref=recv.at[t, e],
            send_sem=ex_send.at[t, e], recv_sem=ex_recv.at[t, e],
            device_id=near[e], device_id_type=MESH,
        )

    def bytes_of(ref, sem):
        return pltpu.make_async_copy(ref, ref, sem)

    def set_weights(e, value):
        weights[rows(e), 0:cols], weights[rows(e), cols:] = halves(value)

    def corner_partials():
        product = dot(cpl_2[...], weights[...])
        product = product[0:16] + product[16:32]
        return product[:, :cols] + product[:, cols:]

    def flex_products(k, e, last=False):
        product = dot(flex_2[e], weights[...])
        product = product[:edge] + product[edge:]
        product = product[:, :cols] + product[:, cols:]
        send[k, e] = product
        if e in (0, 2) or not last:
            pl.when(exists[e])(lambda: edge_copy(k, e).start())
        return colsum(u_ref[e] * product)

    def schur_products(t):
        for e in range(4):
            product = dot(schur_v[rows(e)], weights[...])
            send[t, e] = 0.5 * (product[:, :cols] + product[:, cols:])
            pl.when(exists[e])(lambda e=e: edge_copy(t, e).start())

    def first_stage(k, partial, scalars):
        row_id = iota((8, cols), 0)
        message = partial[0:8]
        for n, value in enumerate(scalars):
            message = jnp.where(row_id == n + 2, value, message)
        own_a[k] = message
        own_b[k] = partial[8:16]
        first[k, i] = message

        @pl.loop(1, nx)
        def _(d):
            pltpu.make_async_remote_copy(
                src_ref=own_a.at[k], dst_ref=first.at[k, i],
                send_sem=f_send.at[k], recv_sem=f_recv.at[k],
                device_id=(lax.rem(i + d, nx), j), device_id_type=MESH,
            ).start()

        @pl.when(j > 0)
        def _():
            @pl.loop(0, nx)
            def _(d):
                pltpu.make_async_remote_copy(
                    src_ref=own_b.at[k], dst_ref=first.at[k, nx + i],
                    send_sem=f_send.at[k], recv_sem=f_recv.at[k],
                    device_id=(lax.rem(i + d, nx), j - 1), device_id_type=MESH,
                ).start()

    def second_stage(k):
        @pl.when(j < ny - 1)
        def _():
            bytes_of(first.at[k, pl.ds(0, 2 * nx - 1)], f_recv.at[k]).wait()

        @pl.when(j == ny - 1)
        def _():
            bytes_of(first.at[k, pl.ds(0, nx - 1)], f_recv.at[k]).wait()

        got_high, got_low = halves(first[k].reshape(2 * nx * 8, cols))
        summed = dot(pick[...], got_high) + dot(pick[...], got_low)
        own_c[k] = summed
        second[k, j] = summed

        @pl.loop(1, ny)
        def _(d):
            pltpu.make_async_remote_copy(
                src_ref=own_c.at[k], dst_ref=second.at[k, j],
                send_sem=g_send.at[k], recv_sem=g_recv.at[k],
                device_id=(i, lax.rem(j + d, ny)), device_id_type=MESH,
            ).start()

    def coarse_solve(k, with_energy):
        bytes_of(second.at[k, pl.ds(0, ny - 1)], g_recv.at[k]).wait()
        gathered = second[k].reshape(kdim, cols)
        g_high, g_low = halves(gathered)
        local = dot3(solve_2[0], solve_2[1], g_high, g_low)
        z_high, z_low = halves(local[0:ZROWS])
        z_ref[0:ZROWS] = z_high
        z_ref[ZROWS : 2 * ZROWS] = z_low
        z_ref[2 * ZROWS :] = z_high
        energy = None
        if with_energy:
            energy = colsum(gathered * dot3(ck_2[0], ck_2[1], g_high, g_low))
        return local[ZROWS : ZROWS + 8], energy

    def scalars_of(k, rz_old, energy_old):
        totals, coarse_part = coarse_solve(k, True)
        rz = totals[0:1]
        beta = jnp.where(k == 1, 0.0, rz / rz_old)
        energy = totals[2:3] + coarse_part + beta * (2.0 * totals[1:2] + beta * energy_old)
        return rz, energy, beta, rz / energy

    def triple(x):
        high, low = halves(x)
        high = high.astype(F32)
        return jnp.concatenate([high, high, low.astype(F32)], 0).T.astype(BF16)

    def precondition_edges(k, t):
        for e in range(4):
            weights[rows(e)] = jnp.zeros((edge, 2 * cols), BF16)

            def arrived(e=e):
                edge_arrival(k, e).wait_recv()
                set_weights(e, 0.5 * (send[k, e] - recv[k, e]))

            pl.when(exists[e])(arrived)
        schur_products(t)

    loads = loads_ref[...]
    weights[:, 0:cols] = loads
    weights[:, cols:] = jnp.zeros_like(loads)
    zero_row = jnp.zeros((1, cols), F32)

    sends_to = (nx - 1) + (ny - 1)

    @pl.when(j > 0)
    def _():
        pl.semaphore_wait(barrier, sends_to + nx - 1)

    @pl.when(j == 0)
    def _():
        pl.semaphore_wait(barrier, sends_to)

    for e in range(4):
        pl.when(exists[e])(lambda e=e: couple_copy(e).start())
    for e in range(4):
        flex_copy(e).wait()
        flex_2[e, 0:edge], flex_2[e, edge:] = halves(flex_v[rows(e)])
        flex_products(0, e)
    first_stage(0, corner_partials(), ())

    coarse_operator()
    for e in range(4):
        b_rows[:, rows(e)] = jnp.zeros((ZROWS, edge), F32)

        def build(e=e):
            couple_arrival(e).wait_recv()
            corner = iota((ZROWS, 8), 0)
            kk = iota((ZROWS, 8), 1)

            def placed(dp, dq):
                at = 6 * (dp + (kk >> 1)) + dq + (kk & 1)
                return jnp.where((corner == at) & (kk < 4), 1.0, 0.0)

            di, dj = NEAR[e]
            b_rows[:, rows(e)] = jnp.dot(placed(2, 2), cown[e], precision=highest) - jnp.dot(
                placed(2 + di, 2 + dj), cnear[e], precision=highest
            )

        pl.when(exists[e])(build)
        bt[rows(e)] = triple(b_rows[:, rows(e)])

    schur_copy.wait()
    precondition_edges(0, ITERS + 1)
    b_high, b_low = halves(b_rows[...])
    contract1 = (((1,), (1,)), ((), ()))
    for e in range(4):
        g_rows[e] = 0.25 * (
            lax.dot_general(b_high, schur_v[rows(e)], contract1, preferred_element_type=F32)
            + lax.dot_general(b_low, schur_v[rows(e)], contract1, preferred_element_type=F32)
        )
        pl.when(exists[e])(lambda e=e: image_copy(e).start())
    second_stage(0)
    for e in range(4):

        def build(e=e):
            image_arrival(e).wait_recv()
            shift = 6 * NEAR[e][0] + NEAR[e][1]
            other = jnp.concatenate([g_near[e, 0:32], jnp.zeros((ZROWS - 32, edge), F32)], 0)
            other = pltpu.roll(other, shift % ZROWS, 0)
            mbt[rows(e)] = triple(g_rows[e] - other)

        pl.when(exists[e])(build)
    coarse_solve(0, False)
    for e in range(4):
        weights[rows(e)] = jnp.zeros((edge, 2 * cols), BF16)

        def arrived(e=e):
            edge_arrival(ITERS + 1, e).wait_recv()
            value = send[ITERS + 1, e] - recv[ITERS + 1, e] + dot(mbt[rows(e)], z_ref[...])
            u_ref[e] = value
            set_weights(e, value)

        pl.when(exists[e])(arrived)

    def open_iteration(k, beta, step, last):
        flex_part = sum(flex_products(k, e, last) for e in range(4))
        for e in range(4):

            def update(e=e):
                image = send[k - 1, e] - recv[k - 1, e] + dot(bt[rows(e)], z_ref[...])
                image = image + beta * s_ref[e]
                s_ref[e] = image
                r_ref[e] = r_ref[e] - step * image

            pl.when(exists[e])(update)
        rz_part = 0.5 * sum(colsum(r_ref[e] * u_ref[e]) for e in range(4))
        cross_part = 0.5 * sum(colsum(s_ref[e] * u_ref[e]) for e in range(4))
        first_stage(k, corner_partials(), (rz_part, cross_part, flex_part))

    def step_along(beta, step):
        for n, e in enumerate((1, 3)):
            direction = u_ref[e] + beta * p_ref[n]
            p_ref[n] = direction
            mult_ref[n] = mult_ref[n] + step * direction

    def iteration(k, carry):
        rz, energy, beta, step = carry
        t = ITERS + 1 + k
        open_iteration(k, beta, step, False)
        precondition_edges(k, t)
        second_stage(k)
        rz, energy, beta, step = scalars_of(k, rz, energy)
        step_along(beta, step)
        for e in range(4):
            weights[rows(e)] = jnp.zeros((edge, 2 * cols), BF16)

            def arrived(e=e):
                edge_arrival(t, e).wait_recv()
                image = send[t, e] - recv[t, e] + dot(mbt[rows(e)], z_ref[...])
                image = image + beta * q_ref[e]
                q_ref[e] = image
                value = u_ref[e] - step * image
                u_ref[e] = value
                set_weights(e, value)

            pl.when(exists[e])(arrived)
        return rz, energy, beta, step

    one_row = zero_row + 1.0
    rz, energy, beta, step = lax.fori_loop(
        1, ITERS, iteration, (one_row, zero_row, zero_row, -one_row)
    )
    open_iteration(ITERS, beta, step, True)
    second_stage(ITERS)
    rz, energy, beta, step = scalars_of(ITERS, rz, energy)
    step_along(beta, step)
    for n, e in enumerate((1, 3)):
        resid_ref[n] = jnp.zeros((edge, cols), F32)

        def arrived(n=n, e=e):
            edge_arrival(ITERS, e).wait_recv()
            image = send[ITERS, e] - recv[ITERS, e] + dot(bt[rows(e)], z_ref[...])
            resid_ref[n] = r_ref[e] - step * (image + beta * s_ref[e])

        pl.when(exists[e])(arrived)

    for e in range(4):

        def sent(e=e):
            couple_copy(e).wait_send()
            image_copy(e).wait_send()

        pl.when(exists[e])(sent)

    @pl.loop(0, 2 * ITERS + 1)
    def _(t):
        for e in range(4):
            if e in (0, 2):
                pl.when(exists[e])(lambda e=e: edge_copy(t, e).wait_send())
            else:
                pl.when(exists[e] & (t != ITERS))(lambda e=e: edge_copy(t, e).wait_send())

    @pl.loop(0, ITERS + 1)
    def _(k):
        @pl.when(j > 0)
        def _():
            bytes_of(first.at[k, pl.ds(0, 2 * nx - 1)], f_send.at[k]).wait()

        @pl.when(j == 0)
        def _():
            bytes_of(first.at[k, pl.ds(0, nx - 1)], f_send.at[k]).wait()

        bytes_of(second.at[k, pl.ds(0, ny - 1)], g_send.at[k]).wait()


def per_device(loads, flex, schur, couple, corner_perm, coarse_inverse):
    nx = lax.axis_size("sx")
    ny = lax.axis_size("sy")
    iface, cols = loads.shape[2:]
    edge = iface // 4
    nc = coarse_inverse.shape[0]
    ncp = -(-nc // 128) * 128
    group = -(-(nx - 1) // 8) * 8 + 8
    kdim = ny * group
    perm = corner_perm.reshape(nx - 1, ny - 1).T
    perm = jnp.pad(perm, ((0, 1), (0, group - (nx - 1))), constant_values=-1).reshape(1, kdim)
    steps = 2 * ITERS + 1
    rounds = ITERS + 1
    vmem = pl.BlockSpec(memory_space=pltpu.VMEM)
    hbm = pl.BlockSpec(memory_space=pl.ANY)
    dma = pltpu.SemaphoreType.DMA
    out = jax.ShapeDtypeStruct((2, edge, cols), F32)
    mult, resid = pl.pallas_call(
        functools.partial(kernel, nx, ny, edge, group),
        out_shape=(out, out),
        in_specs=[vmem, hbm, hbm, vmem, vmem, vmem],
        out_specs=(vmem, vmem),
        scratch_shapes=[
            pltpu.VMEM((iface, iface), F32),
            pltpu.VMEM((4, 2 * edge, iface), BF16),
            pltpu.VMEM((iface, iface), BF16),
            pltpu.VMEM((ncp, ncp), F32),
            pltpu.VMEM((2, kdim, kdim), BF16),
            pltpu.VMEM((2, ZROWS + 8, kdim), BF16),
            pltpu.VMEM((group, 2 * nx * 8), BF16),
            pltpu.VMEM((32, iface), BF16),
            pltpu.VMEM((4, 8, edge), F32),
            pltpu.VMEM((4, 8, edge), F32),
            pltpu.VMEM((ZROWS, iface), F32),
            pltpu.VMEM((iface, 3 * ZROWS), BF16),
            pltpu.VMEM((4, ZROWS, edge), F32),
            pltpu.VMEM((4, ZROWS, edge), F32),
            pltpu.VMEM((iface, 3 * ZROWS), BF16),
            pltpu.VMEM((steps, 4, edge, cols), F32),
            pltpu.VMEM((steps, 4, edge, cols), F32),
            pltpu.VMEM((rounds, 8, cols), F32),
            pltpu.VMEM((rounds, 8, cols), F32),
            pltpu.VMEM((rounds, 2 * nx, 8, cols), F32),
            pltpu.VMEM((rounds, group, cols), F32),
            pltpu.VMEM((rounds, ny, group, cols), F32),
            pltpu.VMEM((4, edge, cols), F32),
            pltpu.VMEM((iface, 2 * cols), BF16),
            pltpu.VMEM((3 * ZROWS, cols), BF16),
            pltpu.VMEM((4, edge, cols), F32),
            pltpu.VMEM((4, edge, cols), F32),
            pltpu.VMEM((4, edge, cols), F32),
            pltpu.VMEM((2, edge, cols), F32),
            dma((4,)),
            dma,
            dma((4,)),
            dma((4,)),
            dma((4,)),
            dma((4,)),
            dma((steps, 4)),
            dma((steps, 4)),
            dma((rounds,)),
            dma((rounds,)),
            dma((rounds,)),
            dma((rounds,)),
        ],
        compiler_params=pltpu.CompilerParams(
            collective_id=0, has_side_effects=True, vmem_limit_bytes=48 * 1024 * 1024
        ),
    )(loads[0, 0], flex[0, 0], schur[0, 0], couple[0, 0], perm, coarse_inverse)
    return mult[None, None], resid[None, None]


def solution(mesh):
    placed = (
        P("sx", "sy", None, None),
        P("sx", "sy", None, None),
        P("sx", "sy", None, None),
        P("sx", "sy", None, None),
        P(),
        P(),
    )
    return jax.shard_map(
        per_device,
        mesh=mesh,
        in_specs=placed,
        out_specs=(P("sx", "sy", None, None, None), P("sx", "sy", None, None, None)),
        check_vma=False,
    )
```

```python
import functools

import jax
import jax.numpy as jnp
from jax import lax
from jax.experimental import pallas as pl
from jax.experimental.pallas import tpu as pltpu
from jax.sharding import PartitionSpec as P

ITERS = 4
ZROWS = 48
MESH = pl.DeviceIdType.MESH
F32 = jnp.float32
BF16 = jnp.bfloat16
OPPOSITE = (1, 0, 3, 2)
NEAR = ((-1, 0), (1, 0), (0, -1), (0, 1))


def dot(a, b):
    return jnp.dot(a, b, preferred_element_type=F32)


def halves(x):
    high = x.astype(BF16)
    return high, (x - high.astype(F32)).astype(BF16)


def dot3(a_high, a_low, b_high, b_low):
    return dot(a_high, b_high) + (dot(a_high, b_low) + dot(a_low, b_high))


def colsum(x):
    return jnp.sum(x, axis=0, keepdims=True)


def iota(shape, dim):
    return lax.broadcasted_iota(jnp.int32, shape, dim)


def kernel(
    nx, ny, edge, group,
    loads_hbm, flex_hbm, schur_hbm, couple_hbm, perm_ref, cinv_hbm,
    mult_ref, resid_ref,
    loads_ref, couple_ref, cinv_ref, flex_v, flex_2, schur_v, cpad, ck_2, solve_2,
    pick, cpl_2, cown, cnear, b_rows, bt, g_rows, g_near, mbt,
    recv, send, own_a, own_b, first, own_c, second,
    u_ref, weights, z_ref, r_ref, s_ref, q_ref, p_ref,
    in_sem, flex_sem, schur_sem, cs_sem, cr_sem, gs_sem, gr_sem,
    ex_send, ex_recv, f_send, f_recv, g_send, g_recv,
):
    i = lax.axis_index("sx")
    j = lax.axis_index("sy")
    exists = (i > 0, i < nx - 1, j > 0, j < ny - 1)
    near = tuple((i + di, j + dj) for di, dj in NEAR)
    kdim = ny * group
    cols = loads_hbm.shape[1]
    highest = lax.Precision.HIGHEST

    def rows(e):
        return pl.ds(e * edge, edge)

    def flex_copy(e):
        return pltpu.make_async_copy(flex_hbm.at[rows(e)], flex_v.at[rows(e)], flex_sem.at[e])

    inputs = tuple(
        pltpu.make_async_copy(source, target, in_sem.at[n])
        for n, (source, target) in enumerate(
            ((couple_hbm, couple_ref), (loads_hbm, loads_ref), (cinv_hbm, cinv_ref))
        )
    )
    for e in range(4):
        flex_copy(e).start()
    barrier = pltpu.get_barrier_semaphore()

    @pl.loop(1, nx, unroll=True)
    def _(d):
        pl.semaphore_signal(barrier, inc=1, device_id=(lax.rem(i + d, nx), j), device_id_type=MESH)

    @pl.when(j < ny - 1)
    def _():
        @pl.loop(0, nx, unroll=True)
        def _(d):
            pl.semaphore_signal(barrier, inc=1, device_id=(d, j + 1), device_id_type=MESH)

    @pl.loop(0, ny, unroll=True)
    def _(d):
        @pl.when((d != j) & (d != j + 1))
        def _():
            pl.semaphore_signal(barrier, inc=1, device_id=(i, d), device_id_type=MESH)

    inputs[0].start()
    inputs[1].start()
    inputs[2].start()
    schur_copy = pltpu.make_async_copy(schur_hbm, schur_v, schur_sem)
    schur_copy.start()

    inputs[0].wait()
    couple_all = couple_ref[...]
    zero6 = jnp.zeros((6, couple_all.shape[1]), F32)
    stacked = jnp.concatenate(
        [couple_all[1:2], couple_all[3:4], zero6, couple_all[0:1], couple_all[2:3], zero6], 0
    )
    cpl_2[0:16], cpl_2[16:32] = halves(stacked)
    for e in range(4):
        cown[e] = jnp.concatenate(
            [couple_all[:, e * edge : (e + 1) * edge], jnp.zeros((4, edge), F32)], 0
        )

    pm = iota(pick.shape, 0)
    pn = iota(pick.shape, 1)
    slot = pn >> 3
    row = pn & 7
    source = slot - jnp.where(slot >= nx, nx, 0)
    corner_row = (pm < nx - 1) & (row < 2) & (source + row == pm + 1)
    scalar_row = (pm >= group - 8) & (slot < nx) & (row >= 2) & (row - 2 == pm - (group - 8))
    pick[...] = jnp.where(corner_row | scalar_row, 1.0, 0.0).astype(BF16)

    for ref in (r_ref, s_ref, q_ref, p_ref, mult_ref, u_ref):
        ref[...] = jnp.zeros_like(ref)

    @pl.when(j == ny - 1)
    def _():
        first[:, nx:, :, :] = jnp.zeros((ITERS + 1, nx, 8, cols), F32)

    def coarse_operator():
        inputs[2].wait()
        nc = cinv_ref.shape[0]
        cpad[...] = jnp.zeros_like(cpad)
        cpad[0:nc, 0:nc] = cinv_ref[...]
        ncp = cpad.shape[0]
        numbered = jnp.where(iota((ncp, nc), 0) == perm_ref[...], 1.0, 0.0).astype(BF16)
        place = iota((nc, kdim), 1)
        place_q = (place * (65536 // group + 1)) >> 16
        place_p = place - group * place_q
        lies = (place_p < nx - 1) & (place_q < ny - 1)
        lies = lies & (iota((nc, kdim), 0) == place_p * (ny - 1) + place_q)
        order = dot(numbered, jnp.where(lies, 1.0, 0.0).astype(BF16)).astype(BF16)
        m_id = iota((ZROWS + 8, kdim), 0)
        col = iota((ZROWS + 8, kdim), 1)
        block_row = (m_id * 43) >> 8
        corner_p = i - 2 + block_row
        corner_q = j - 2 + m_id - 6 * block_row
        inside = (m_id < 36) & (corner_p >= 1) & (corner_p <= nx - 1)
        inside = inside & (corner_q >= 1) & (corner_q <= ny - 1)
        wanted = group * (corner_q - 1) + corner_p - 1
        select = jnp.where(inside & (col == wanted), 1.0, 0.0).astype(BF16)
        col_in = col - group * ((col * (65536 // group + 1)) >> 16)
        totals = jnp.where((m_id >= ZROWS) & (col_in == m_id - ZROWS + group - 8), 1.0, 0.0)
        contract0 = (((0,), (0,)), ((), ()))
        for n, part in enumerate(halves(cpad[...])):
            right = dot(part, order).astype(BF16)
            full = lax.dot_general(order, right, contract0, preferred_element_type=F32).astype(BF16)
            ck_2[n] = full
            solve_2[n] = (dot(select, full) + (totals if n == 0 else 0.0)).astype(BF16)

    def couple_copy(e):
        return pltpu.make_async_remote_copy(
            src_ref=cown.at[e], dst_ref=cnear.at[OPPOSITE[e]],
            send_sem=cs_sem.at[e], recv_sem=cr_sem.at[OPPOSITE[e]],
            device_id=near[e], device_id_type=MESH,
        )

    def couple_arrival(e):
        return pltpu.make_async_remote_copy(
            src_ref=cown.at[e], dst_ref=cnear.at[e],
            send_sem=cs_sem.at[e], recv_sem=cr_sem.at[e],
            device_id=near[e], device_id_type=MESH,
        )

    def image_copy(e):
        return pltpu.make_async_remote_copy(
            src_ref=g_rows.at[e, pl.ds(0, 32)], dst_ref=g_near.at[OPPOSITE[e], pl.ds(0, 32)],
            send_sem=gs_sem.at[e], recv_sem=gr_sem.at[OPPOSITE[e]],
            device_id=near[e], device_id_type=MESH,
        )

    def image_arrival(e):
        return pltpu.make_async_remote_copy(
            src_ref=g_rows.at[e, pl.ds(0, 32)], dst_ref=g_near.at[e, pl.ds(0, 32)],
            send_sem=gs_sem.at[e], recv_sem=gr_sem.at[e],
            device_id=near[e], device_id_type=MESH,
        )

    def edge_copy(t, e):
        return pltpu.make_async_remote_copy(
            src_ref=send.at[t, e], dst_ref=recv.at[t, OPPOSITE[e]],
            send_sem=ex_send.at[t, e], recv_sem=ex_recv.at[t, OPPOSITE[e]],
            device_id=near[e], device_id_type=MESH,
        )

    def edge_arrival(t, e):
        return pltpu.make_async_remote_copy(
            src_ref=send.at[t, e], dst_ref=recv.at[t, e],
            send_sem=ex_send.at[t, e], recv_sem=ex_recv.at[t, e],
            device_id=near[e], device_id_type=MESH,
        )

    def bytes_of(ref, sem):
        return pltpu.make_async_copy(ref, ref, sem)

    def set_weights(e, value):
        weights[rows(e), 0:cols], weights[rows(e), cols:] = halves(value)

    def corner_partials():
        product = dot(cpl_2[...], weights[...])
        product = product[0:16] + product[16:32]
        return product[:, :cols] + product[:, cols:]

    def flex_products(k, e):
        product = dot(flex_2[e], weights[...])
        product = product[:edge] + product[edge:]
        product = product[:, :cols] + product[:, cols:]
        send[k, e] = product
        return colsum(u_ref[e] * product)

    def send_edges(k, last=False):
        for e in range(4):
            if e in (0, 2) or not last:
                pl.when(exists[e])(lambda e=e: edge_copy(k, e).start())

    def schur_products(t):
        for e in range(4):
            product = dot(schur_v[rows(e)], weights[...])
            send[t, e] = 0.5 * (product[:, :cols] + product[:, cols:])
            pl.when(exists[e])(lambda e=e: edge_copy(t, e).start())

    def first_stage(k, partial, scalars):
        row_id = iota((8, cols), 0)
        message = partial[0:8]
        for n, value in enumerate(scalars):
            message = jnp.where(row_id == n + 2, value, message)
        own_a[k] = message
        own_b[k] = partial[8:16]
        first[k, i] = message

        @pl.loop(0, nx, unroll=True)
        def _(n):
            d = lax.rem(n + 1 + nx // 4, nx)
            to = lax.rem(i + d, nx)

            @pl.when(j > 0)
            def _():
                pltpu.make_async_remote_copy(
                    src_ref=own_b.at[k], dst_ref=first.at[k, nx + i],
                    send_sem=f_send.at[k], recv_sem=f_recv.at[k],
                    device_id=(to, j - 1), device_id_type=MESH,
                ).start()

            @pl.when(d != 0)
            def _():
                pltpu.make_async_remote_copy(
                    src_ref=own_a.at[k], dst_ref=first.at[k, i],
                    send_sem=f_send.at[k], recv_sem=f_recv.at[k],
                    device_id=(to, j), device_id_type=MESH,
                ).start()

    def second_stage(k):
        @pl.when(j < ny - 1)
        def _():
            bytes_of(first.at[k, pl.ds(0, 2 * nx - 1)], f_recv.at[k]).wait()

        @pl.when(j == ny - 1)
        def _():
            bytes_of(first.at[k, pl.ds(0, nx - 1)], f_recv.at[k]).wait()

        got_high, got_low = halves(first[k].reshape(2 * nx * 8, cols))
        summed = dot(pick[...], got_high) + dot(pick[...], got_low)
        own_c[k] = summed
        second[k, j] = summed

        @pl.loop(0, ny - 1, unroll=True)
        def _(n):
            d = 1 + lax.rem(n + ny // 4, ny - 1)
            pltpu.make_async_remote_copy(
                src_ref=own_c.at[k], dst_ref=second.at[k, j],
                send_sem=g_send.at[k], recv_sem=g_recv.at[k],
                device_id=(i, lax.rem(j + d, ny)), device_id_type=MESH,
            ).start()

    def coarse_solve(k, with_energy):
        bytes_of(second.at[k, pl.ds(0, ny - 1)], g_recv.at[k]).wait()
        gathered = second[k].reshape(kdim, cols)
        g_high, g_low = halves(gathered)
        local = dot3(solve_2[0], solve_2[1], g_high, g_low)
        z_high, z_low = halves(local[0:ZROWS])
        z_ref[0:ZROWS] = z_high
        z_ref[ZROWS : 2 * ZROWS] = z_low
        z_ref[2 * ZROWS :] = z_high
        energy = None
        if with_energy:
            energy = colsum(gathered * dot3(ck_2[0], ck_2[1], g_high, g_low))
        return local[ZROWS : ZROWS + 8], energy

    def scalars_of(k, rz_old, energy_old):
        totals, coarse_part = coarse_solve(k, True)
        rz = totals[0:1]
        beta = jnp.where(k == 1, 0.0, rz / rz_old)
        energy = totals[2:3] + coarse_part + beta * (2.0 * totals[1:2] + beta * energy_old)
        return rz, energy, beta, rz / energy

    def triple(x):
        high, low = halves(x)
        high = high.astype(F32)
        return jnp.concatenate([high, high, low.astype(F32)], 0).T.astype(BF16)

    def precondition_edges(k, t):
        for e in range(4):
            weights[rows(e)] = jnp.zeros((edge, 2 * cols), BF16)

            def arrived(e=e):
                edge_arrival(k, e).wait_recv()
                set_weights(e, 0.5 * (send[k, e] - recv[k, e]))

            pl.when(exists[e])(arrived)
        schur_products(t)

    def update_residual(k, beta, step):
        for e in range(4):

            def update(e=e):
                image = send[k, e] - recv[k, e] + dot(bt[rows(e)], z_ref[...])
                image = image + beta * s_ref[e]
                s_ref[e] = image
                r_ref[e] = r_ref[e] - step * image

            pl.when(exists[e])(update)

    def open_iteration(k, last):
        flex_part = sum(flex_products(k, e) for e in range(4))
        rz_part = 0.5 * sum(colsum(r_ref[e] * u_ref[e]) for e in range(4))
        cross_part = 0.5 * sum(colsum(s_ref[e] * u_ref[e]) for e in range(4))
        first_stage(k, corner_partials(), (rz_part, cross_part, flex_part))
        send_edges(k, last)

    inputs[1].wait()
    loads = loads_ref[...]
    weights[:, 0:cols] = loads
    weights[:, cols:] = jnp.zeros_like(loads)
    zero_row = jnp.zeros((1, cols), F32)

    for e in range(4):
        flex_copy(e).wait()
        flex_2[e, 0:edge], flex_2[e, edge:] = halves(flex_v[rows(e)])
        flex_products(0, e)
    partial = corner_partials()

    sends_to = (nx - 1) + (ny - 1)

    @pl.when(j > 0)
    def _():
        pl.semaphore_wait(barrier, sends_to + nx - 1)

    @pl.when(j == 0)
    def _():
        pl.semaphore_wait(barrier, sends_to)

    first_stage(0, partial, ())
    for e in range(4):
        pl.when(exists[e])(lambda e=e: couple_copy(e).start())
    send_edges(0)

    coarse_operator()
    for e in range(4):
        b_rows[:, rows(e)] = jnp.zeros((ZROWS, edge), F32)

        def build(e=e):
            couple_arrival(e).wait_recv()
            corner = iota((ZROWS, 8), 0)
            kk = iota((ZROWS, 8), 1)

            def placed(dp, dq):
                at = 6 * (dp + (kk >> 1)) + dq + (kk & 1)
                return jnp.where((corner == at) & (kk < 4), 1.0, 0.0)

            di, dj = NEAR[e]
            b_rows[:, rows(e)] = jnp.dot(placed(2, 2), cown[e], precision=highest) - jnp.dot(
                placed(2 + di, 2 + dj), cnear[e], precision=highest
            )

        pl.when(exists[e])(build)
        bt[rows(e)] = triple(b_rows[:, rows(e)])

    schur_copy.wait()
    b_high, b_low = halves(b_rows[...])
    contract1 = (((1,), (1,)), ((), ()))
    for e in range(4):
        g_rows[e] = 0.25 * (
            lax.dot_general(b_high, schur_v[rows(e)], contract1, preferred_element_type=F32)
            + lax.dot_general(b_low, schur_v[rows(e)], contract1, preferred_element_type=F32)
        )
        pl.when(exists[e])(lambda e=e: image_copy(e).start())
    second_stage(0)
    precondition_edges(0, ITERS + 1)
    for e in range(4):

        def build(e=e):
            image_arrival(e).wait_recv()
            shift = 6 * NEAR[e][0] + NEAR[e][1]
            other = jnp.concatenate([g_near[e, 0:32], jnp.zeros((ZROWS - 32, edge), F32)], 0)
            other = pltpu.roll(other, shift % ZROWS, 0)
            mbt[rows(e)] = triple(g_rows[e] - other)

        pl.when(exists[e])(build)
    coarse_solve(0, False)
    one_row = zero_row + 1.0
    update_residual(0, zero_row, -one_row)
    for e in range(4):
        weights[rows(e)] = jnp.zeros((edge, 2 * cols), BF16)

        def arrived(e=e):
            edge_arrival(ITERS + 1, e).wait_recv()
            value = send[ITERS + 1, e] - recv[ITERS + 1, e] + dot(mbt[rows(e)], z_ref[...])
            u_ref[e] = value
            set_weights(e, value)

        pl.when(exists[e])(arrived)

    def step_along(beta, step):
        for n, e in enumerate((1, 3)):
            direction = u_ref[e] + beta * p_ref[n]
            p_ref[n] = direction
            mult_ref[n] = mult_ref[n] + step * direction

    def iteration(k, carry):
        t = ITERS + 1 + k
        open_iteration(k, False)
        second_stage(k)
        precondition_edges(k, t)
        rz, energy, beta, step = scalars_of(k, *carry)
        step_along(beta, step)
        update_residual(k, beta, step)
        for e in range(4):
            weights[rows(e)] = jnp.zeros((edge, 2 * cols), BF16)

            def arrived(e=e):
                edge_arrival(t, e).wait_recv()
                image = send[t, e] - recv[t, e] + dot(mbt[rows(e)], z_ref[...])
                image = image + beta * q_ref[e]
                q_ref[e] = image
                value = u_ref[e] - step * image
                u_ref[e] = value
                set_weights(e, value)

            pl.when(exists[e])(arrived)
        return rz, energy

    rz, energy = lax.fori_loop(1, ITERS, iteration, (one_row, zero_row))
    open_iteration(ITERS, True)
    second_stage(ITERS)
    rz, energy, beta, step = scalars_of(ITERS, rz, energy)
    step_along(beta, step)
    for n, e in enumerate((1, 3)):
        resid_ref[n] = jnp.zeros((edge, cols), F32)

        def arrived(n=n, e=e):
            edge_arrival(ITERS, e).wait_recv()
            image = send[ITERS, e] - recv[ITERS, e] + dot(bt[rows(e)], z_ref[...])
            resid_ref[n] = r_ref[e] - step * (image + beta * s_ref[e])

        pl.when(exists[e])(arrived)

    for e in range(4):

        def sent(e=e):
            couple_copy(e).wait_send()
            image_copy(e).wait_send()

        pl.when(exists[e])(sent)

    @pl.loop(0, 2 * ITERS + 1)
    def _(t):
        for e in range(4):
            if e in (0, 2):
                pl.when(exists[e])(lambda e=e: edge_copy(t, e).wait_send())
            else:
                pl.when(exists[e] & (t != ITERS))(lambda e=e: edge_copy(t, e).wait_send())

    @pl.loop(0, ITERS + 1)
    def _(k):
        @pl.when(j > 0)
        def _():
            bytes_of(first.at[k, pl.ds(0, 2 * nx - 1)], f_send.at[k]).wait()

        @pl.when(j == 0)
        def _():
            bytes_of(first.at[k, pl.ds(0, nx - 1)], f_send.at[k]).wait()

        bytes_of(second.at[k, pl.ds(0, ny - 1)], g_send.at[k]).wait()


def per_device(loads, flex, schur, couple, corner_perm, coarse_inverse):
    nx = lax.axis_size("sx")
    ny = lax.axis_size("sy")
    iface, cols = loads.shape[2:]
    edge = iface // 4
    nc = coarse_inverse.shape[0]
    ncp = -(-nc // 128) * 128
    group = -(-(nx - 1) // 8) * 8 + 8
    kdim = ny * group
    steps = 2 * ITERS + 1
    rounds = ITERS + 1
    vmem = pl.BlockSpec(memory_space=pltpu.VMEM)
    hbm = pl.BlockSpec(memory_space=pl.ANY)
    dma = pltpu.SemaphoreType.DMA
    out = jax.ShapeDtypeStruct((2, edge, cols), F32)
    mult, resid = pl.pallas_call(
        functools.partial(kernel, nx, ny, edge, group),
        out_shape=(out, out),
        in_specs=[hbm, hbm, hbm, hbm, vmem, hbm],
        out_specs=(vmem, vmem),
        scratch_shapes=[
            pltpu.VMEM((iface, cols), BF16),
            pltpu.VMEM((4, iface), F32),
            pltpu.VMEM((nc, nc), F32),
            pltpu.VMEM((iface, iface), F32),
            pltpu.VMEM((4, 2 * edge, iface), BF16),
            pltpu.VMEM((iface, iface), BF16),
            pltpu.VMEM((ncp, ncp), F32),
            pltpu.VMEM((2, kdim, kdim), BF16),
            pltpu.VMEM((2, ZROWS + 8, kdim), BF16),
            pltpu.VMEM((group, 2 * nx * 8), BF16),
            pltpu.VMEM((32, iface), BF16),
            pltpu.VMEM((4, 8, edge), F32),
            pltpu.VMEM((4, 8, edge), F32),
            pltpu.VMEM((ZROWS, iface), F32),
            pltpu.VMEM((iface, 3 * ZROWS), BF16),
            pltpu.VMEM((4, ZROWS, edge), F32),
            pltpu.VMEM((4, ZROWS, edge), F32),
            pltpu.VMEM((iface, 3 * ZROWS), BF16),
            pltpu.VMEM((steps, 4, edge, cols), F32),
            pltpu.VMEM((steps, 4, edge, cols), F32),
            pltpu.VMEM((rounds, 8, cols), F32),
            pltpu.VMEM((rounds, 8, cols), F32),
            pltpu.VMEM((rounds, 2 * nx, 8, cols), F32),
            pltpu.VMEM((rounds, group, cols), F32),
            pltpu.VMEM((rounds, ny, group, cols), F32),
            pltpu.VMEM((4, edge, cols), F32),
            pltpu.VMEM((iface, 2 * cols), BF16),
            pltpu.VMEM((3 * ZROWS, cols), BF16),
            pltpu.VMEM((4, edge, cols), F32),
            pltpu.VMEM((4, edge, cols), F32),
            pltpu.VMEM((4, edge, cols), F32),
            pltpu.VMEM((2, edge, cols), F32),
            dma((3,)),
            dma((4,)),
            dma,
            dma((4,)),
            dma((4,)),
            dma((4,)),
            dma((4,)),
            dma((steps, 4)),
            dma((steps, 4)),
            dma((rounds,)),
            dma((rounds,)),
            dma((rounds,)),
            dma((rounds,)),
        ],
        compiler_params=pltpu.CompilerParams(
            collective_id=0, has_side_effects=True, vmem_limit_bytes=60 * 1024 * 1024
        ),
    )(loads[0, 0], flex[0, 0], schur[0, 0], couple[0, 0], corner_perm.reshape(1, nc), coarse_inverse)
    return mult[None, None], resid[None, None]


def solution(mesh):
    placed = (
        P("sx", "sy", None, None),
        P("sx", "sy", None, None),
        P("sx", "sy", None, None),
        P("sx", "sy", None, None),
        P(),
        P(),
    )
    return jax.shard_map(
        per_device,
        mesh=mesh,
        in_specs=placed,
        out_specs=(P("sx", "sy", None, None, None), P("sx", "sy", None, None, None)),
        check_vma=False,
    )
```

```python
import functools

import jax
import jax.numpy as jnp
from jax import lax
from jax.experimental import pallas as pl
from jax.experimental.pallas import tpu as pltpu
from jax.sharding import PartitionSpec as P

ITERS = 4
ZROWS = 48
MESH = pl.DeviceIdType.MESH
F32 = jnp.float32
BF16 = jnp.bfloat16
OPPOSITE = (1, 0, 3, 2)
NEAR = ((-1, 0), (1, 0), (0, -1), (0, 1))


def dot(a, b):
    return jnp.dot(a, b, preferred_element_type=F32)


def halves(x):
    high = x.astype(BF16)
    return high, (x - high.astype(F32)).astype(BF16)


def dot3(a_high, a_low, b_high, b_low):
    return dot(a_high, b_high) + (dot(a_high, b_low) + dot(a_low, b_high))


def colsum(x):
    return jnp.sum(x, axis=0, keepdims=True)


def iota(shape, dim):
    return lax.broadcasted_iota(jnp.int32, shape, dim)


def kernel(
    nx, ny, edge, group,
    loads_hbm, flex_hbm, schur_hbm, couple_hbm, perm_ref, cinv_hbm,
    mult_ref, resid_ref,
    loads_ref, couple_ref, cinv_ref, flex_v, flex_2, schur_v, cpad, ck_2, solve_2,
    pick, cpl_2, cown, cnear, b_rows, bt, g_rows, g_near, mbt,
    recv, send, own_a, own_b, first, own_c, second,
    u_ref, weights, z_ref, r_ref, s_ref, q_ref, p_ref,
    in_sem, flex_sem, schur_sem, cs_sem, cr_sem, gs_sem, gr_sem,
    ex_send, ex_recv, f_send, f_recv, g_send, g_recv,
):
    i = lax.axis_index("sx")
    j = lax.axis_index("sy")
    exists = (i > 0, i < nx - 1, j > 0, j < ny - 1)
    near = tuple((i + di, j + dj) for di, dj in NEAR)
    kdim = ny * group
    cols = loads_hbm.shape[1]
    highest = lax.Precision.HIGHEST

    def rows(e):
        return pl.ds(e * edge, edge)

    def flex_copy(e):
        return pltpu.make_async_copy(flex_hbm.at[rows(e)], flex_v.at[rows(e)], flex_sem.at[e])

    inputs = tuple(
        pltpu.make_async_copy(source, target, in_sem.at[n])
        for n, (source, target) in enumerate(
            ((couple_hbm, couple_ref), (loads_hbm, loads_ref), (cinv_hbm, cinv_ref))
        )
    )
    for e in range(4):
        flex_copy(e).start()
    barrier = pltpu.get_barrier_semaphore()

    @pl.loop(1, nx, unroll=True)
    def _(d):
        pl.semaphore_signal(barrier, inc=1, device_id=(lax.rem(i + d, nx), j), device_id_type=MESH)

    @pl.when(j < ny - 1)
    def _():
        @pl.loop(0, nx, unroll=True)
        def _(d):
            pl.semaphore_signal(barrier, inc=1, device_id=(d, j + 1), device_id_type=MESH)

    @pl.loop(0, ny, unroll=True)
    def _(d):
        @pl.when((d != j) & (d != j + 1))
        def _():
            pl.semaphore_signal(barrier, inc=1, device_id=(i, d), device_id_type=MESH)

    inputs[0].start()
    inputs[1].start()
    inputs[2].start()
    schur_copy = pltpu.make_async_copy(schur_hbm, schur_v, schur_sem)
    schur_copy.start()

    inputs[0].wait()
    couple_all = couple_ref[...]
    zero6 = jnp.zeros((6, couple_all.shape[1]), F32)
    stacked = jnp.concatenate(
        [couple_all[1:2], couple_all[3:4], zero6, couple_all[0:1], couple_all[2:3], zero6], 0
    )
    cpl_2[0:16], cpl_2[16:32] = halves(stacked)
    for e in range(4):
        cown[e] = jnp.concatenate(
            [couple_all[:, e * edge : (e + 1) * edge], jnp.zeros((4, edge), F32)], 0
        )

    pm = iota(pick.shape, 0)
    pn = iota(pick.shape, 1)
    slot = pn >> 3
    row = pn & 7
    source = slot - jnp.where(slot >= nx, nx, 0)
    corner_row = (pm < nx - 1) & (row < 2) & (source + row == pm + 1)
    scalar_row = (pm >= group - 8) & (slot < nx) & (row >= 2) & (row - 2 == pm - (group - 8))
    pick[...] = jnp.where(corner_row | scalar_row, 1.0, 0.0).astype(BF16)

    for ref in (r_ref, s_ref, q_ref, p_ref, mult_ref, u_ref):
        ref[...] = jnp.zeros_like(ref)

    @pl.when(j == ny - 1)
    def _():
        first[:, nx:, :, :] = jnp.zeros((ITERS + 1, nx, 8, cols), F32)

    def coarse_operator():
        inputs[2].wait()
        nc = cinv_ref.shape[0]
        cpad[...] = jnp.zeros_like(cpad)
        cpad[0:nc, 0:nc] = cinv_ref[...]
        ncp = cpad.shape[0]
        numbered = jnp.where(iota((ncp, nc), 0) == perm_ref[...], 1.0, 0.0).astype(BF16)
        place = iota((nc, kdim), 1)
        place_q = (place * (65536 // group + 1)) >> 16
        place_p = place - group * place_q
        lies = (place_p < nx - 1) & (place_q < ny - 1)
        lies = lies & (iota((nc, kdim), 0) == place_p * (ny - 1) + place_q)
        order = dot(numbered, jnp.where(lies, 1.0, 0.0).astype(BF16)).astype(BF16)
        m_id = iota((ZROWS + 8, kdim), 0)
        col = iota((ZROWS + 8, kdim), 1)
        block_row = (m_id * 43) >> 8
        corner_p = i - 2 + block_row
        corner_q = j - 2 + m_id - 6 * block_row
        inside = (m_id < 36) & (corner_p >= 1) & (corner_p <= nx - 1)
        inside = inside & (corner_q >= 1) & (corner_q <= ny - 1)
        wanted = group * (corner_q - 1) + corner_p - 1
        select = jnp.where(inside & (col == wanted), 1.0, 0.0).astype(BF16)
        col_in = col - group * ((col * (65536 // group + 1)) >> 16)
        totals = jnp.where((m_id >= ZROWS) & (col_in == m_id - ZROWS + group - 8), 1.0, 0.0)
        contract0 = (((0,), (0,)), ((), ()))
        for n, part in enumerate(halves(cpad[...])):
            right = dot(part, order).astype(BF16)
            full = lax.dot_general(order, right, contract0, preferred_element_type=F32).astype(BF16)
            ck_2[n] = full
            solve_2[n] = (dot(select, full) + (totals if n == 0 else 0.0)).astype(BF16)

    def couple_copy(e):
        return pltpu.make_async_remote_copy(
            src_ref=cown.at[e], dst_ref=cnear.at[OPPOSITE[e]],
            send_sem=cs_sem.at[e], recv_sem=cr_sem.at[OPPOSITE[e]],
            device_id=near[e], device_id_type=MESH,
        )

    def couple_arrival(e):
        return pltpu.make_async_remote_copy(
            src_ref=cown.at[e], dst_ref=cnear.at[e],
            send_sem=cs_sem.at[e], recv_sem=cr_sem.at[e],
            device_id=near[e], device_id_type=MESH,
        )

    def image_copy(e):
        return pltpu.make_async_remote_copy(
            src_ref=g_rows.at[e, pl.ds(0, 32)], dst_ref=g_near.at[OPPOSITE[e], pl.ds(0, 32)],
            send_sem=gs_sem.at[e], recv_sem=gr_sem.at[OPPOSITE[e]],
            device_id=near[e], device_id_type=MESH,
        )

    def image_arrival(e):
        return pltpu.make_async_remote_copy(
            src_ref=g_rows.at[e, pl.ds(0, 32)], dst_ref=g_near.at[e, pl.ds(0, 32)],
            send_sem=gs_sem.at[e], recv_sem=gr_sem.at[e],
            device_id=near[e], device_id_type=MESH,
        )

    def edge_copy(t, e):
        return pltpu.make_async_remote_copy(
            src_ref=send.at[t, e], dst_ref=recv.at[t, OPPOSITE[e]],
            send_sem=ex_send.at[t, e], recv_sem=ex_recv.at[t, OPPOSITE[e]],
            device_id=near[e], device_id_type=MESH,
        )

    def edge_arrival(t, e):
        return pltpu.make_async_remote_copy(
            src_ref=send.at[t, e], dst_ref=recv.at[t, e],
            send_sem=ex_send.at[t, e], recv_sem=ex_recv.at[t, e],
            device_id=near[e], device_id_type=MESH,
        )

    def bytes_of(ref, sem):
        return pltpu.make_async_copy(ref, ref, sem)

    def set_weights(e, value):
        weights[rows(e), 0:cols], weights[rows(e), cols:] = halves(value)

    def corner_partials():
        product = dot(cpl_2[...], weights[...])
        product = product[0:16] + product[16:32]
        return product[:, :cols] + product[:, cols:]

    def flex_products(k, e):
        product = dot(flex_2[e], weights[:, 0:cols])
        product = product[:edge] + product[edge:]
        send[k, e] = product
        return colsum(u_ref[e] * product)

    def send_edges(k, last=False):
        for e in range(4):
            if e in (0, 2) or not last:
                pl.when(exists[e])(lambda e=e: edge_copy(k, e).start())

    def schur_products(t):
        for e in range(4):
            product = dot(schur_v[rows(e)], weights[...])
            send[t, e] = 0.5 * (product[:, :cols] + product[:, cols:])
            pl.when(exists[e])(lambda e=e: edge_copy(t, e).start())

    def first_stage(k, partial, scalars):
        row_id = iota((8, cols), 0)
        message = partial[0:8]
        for n, value in enumerate(scalars):
            message = jnp.where(row_id == n + 2, value, message)
        own_a[k] = message
        own_b[k] = partial[8:16]
        first[k, i] = message

        @pl.loop(0, nx, unroll=True)
        def _(n):
            d = lax.rem(n + 1 + nx // 4, nx)
            to = lax.rem(i + d, nx)

            @pl.when(j > 0)
            def _():
                pltpu.make_async_remote_copy(
                    src_ref=own_b.at[k], dst_ref=first.at[k, nx + i],
                    send_sem=f_send.at[k], recv_sem=f_recv.at[k],
                    device_id=(to, j - 1), device_id_type=MESH,
                ).start()

            @pl.when(d != 0)
            def _():
                pltpu.make_async_remote_copy(
                    src_ref=own_a.at[k], dst_ref=first.at[k, i],
                    send_sem=f_send.at[k], recv_sem=f_recv.at[k],
                    device_id=(to, j), device_id_type=MESH,
                ).start()

    def second_stage(k):
        @pl.when(j < ny - 1)
        def _():
            bytes_of(first.at[k, pl.ds(0, 2 * nx - 1)], f_recv.at[k]).wait()

        @pl.when(j == ny - 1)
        def _():
            bytes_of(first.at[k, pl.ds(0, nx - 1)], f_recv.at[k]).wait()

        got_high, got_low = halves(first[k].reshape(2 * nx * 8, cols))
        summed = dot(pick[...], got_high) + dot(pick[...], got_low)
        own_c[k] = summed
        second[k, j] = summed

        @pl.loop(0, ny - 1, unroll=True)
        def _(n):
            d = 1 + lax.rem(n + ny // 4, ny - 1)
            pltpu.make_async_remote_copy(
                src_ref=own_c.at[k], dst_ref=second.at[k, j],
                send_sem=g_send.at[k], recv_sem=g_recv.at[k],
                device_id=(i, lax.rem(j + d, ny)), device_id_type=MESH,
            ).start()

    def coarse_solve(k, with_energy):
        bytes_of(second.at[k, pl.ds(0, ny - 1)], g_recv.at[k]).wait()
        gathered = second[k].reshape(kdim, cols)
        g_high, g_low = halves(gathered)
        local = dot3(solve_2[0], solve_2[1], g_high, g_low)
        z_high, z_low = halves(local[0:ZROWS])
        z_ref[0:ZROWS] = z_high
        z_ref[ZROWS : 2 * ZROWS] = z_low
        z_ref[2 * ZROWS :] = z_high
        energy = None
        if with_energy:
            energy = colsum(gathered * dot3(ck_2[0], ck_2[1], g_high, g_low))
        return local[ZROWS : ZROWS + 8], energy

    def scalars_of(k, rz_old, energy_old):
        totals, coarse_part = coarse_solve(k, True)
        rz = totals[0:1]
        beta = jnp.where(k == 1, 0.0, rz / rz_old)
        energy = totals[2:3] + coarse_part + beta * (2.0 * totals[1:2] + beta * energy_old)
        return rz, energy, beta, rz / energy

    def triple(x):
        high, low = halves(x)
        high = high.astype(F32)
        return jnp.concatenate([high, high, low.astype(F32)], 0).T.astype(BF16)

    def precondition_edges(k, t):
        for e in range(4):
            weights[rows(e)] = jnp.zeros((edge, 2 * cols), BF16)

            def arrived(e=e):
                edge_arrival(k, e).wait_recv()
                set_weights(e, 0.5 * (send[k, e] - recv[k, e]))

            pl.when(exists[e])(arrived)
        schur_products(t)

    def update_residual(k, beta, step):
        for e in range(4):

            def update(e=e):
                image = send[k, e] - recv[k, e] + dot(bt[rows(e)], z_ref[...])
                image = image + beta * s_ref[e]
                s_ref[e] = image
                r_ref[e] = r_ref[e] - step * image

            pl.when(exists[e])(update)

    def open_iteration(k, last):
        flex_part = sum(flex_products(k, e) for e in range(4))
        rz_part = 0.5 * sum(colsum(r_ref[e] * u_ref[e]) for e in range(4))
        cross_part = 0.5 * sum(colsum(s_ref[e] * u_ref[e]) for e in range(4))
        first_stage(k, corner_partials(), (rz_part, cross_part, flex_part))
        send_edges(k, last)

    inputs[1].wait()
    loads = loads_ref[...]
    weights[:, 0:cols] = loads
    weights[:, cols:] = jnp.zeros_like(loads)
    zero_row = jnp.zeros((1, cols), F32)

    for e in range(4):
        flex_copy(e).wait()
        flex_2[e, 0:edge], flex_2[e, edge:] = halves(flex_v[rows(e)])
        flex_products(0, e)
    partial = corner_partials()

    sends_to = (nx - 1) + (ny - 1)

    @pl.when(j > 0)
    def _():
        pl.semaphore_wait(barrier, sends_to + nx - 1)

    @pl.when(j == 0)
    def _():
        pl.semaphore_wait(barrier, sends_to)

    first_stage(0, partial, ())
    for e in range(4):
        pl.when(exists[e])(lambda e=e: couple_copy(e).start())
    send_edges(0)

    coarse_operator()
    for e in range(4):
        b_rows[:, rows(e)] = jnp.zeros((ZROWS, edge), F32)

        def build(e=e):
            couple_arrival(e).wait_recv()
            corner = iota((ZROWS, 8), 0)
            kk = iota((ZROWS, 8), 1)

            def placed(dp, dq):
                at = 6 * (dp + (kk >> 1)) + dq + (kk & 1)
                return jnp.where((corner == at) & (kk < 4), 1.0, 0.0)

            di, dj = NEAR[e]
            b_rows[:, rows(e)] = jnp.dot(placed(2, 2), cown[e], precision=highest) - jnp.dot(
                placed(2 + di, 2 + dj), cnear[e], precision=highest
            )

        pl.when(exists[e])(build)
        bt[rows(e)] = triple(b_rows[:, rows(e)])

    schur_copy.wait()
    b_both = jnp.concatenate(halves(b_rows[...]), 0)
    contract1 = (((1,), (1,)), ((), ()))
    for e in range(4):
        product = lax.dot_general(
            b_both, schur_v[rows(e)], contract1, preferred_element_type=F32
        )
        g_rows[e] = 0.25 * (product[:ZROWS] + product[ZROWS:])
        pl.when(exists[e])(lambda e=e: image_copy(e).start())
    second_stage(0)
    precondition_edges(0, ITERS + 1)
    for e in range(4):

        def build(e=e):
            image_arrival(e).wait_recv()
            shift = 6 * NEAR[e][0] + NEAR[e][1]
            other = jnp.concatenate([g_near[e, 0:32], jnp.zeros((ZROWS - 32, edge), F32)], 0)
            other = pltpu.roll(other, shift % ZROWS, 0)
            mbt[rows(e)] = triple(g_rows[e] - other)

        pl.when(exists[e])(build)
    coarse_solve(0, False)
    one_row = zero_row + 1.0
    update_residual(0, zero_row, -one_row)
    for e in range(4):
        weights[rows(e)] = jnp.zeros((edge, 2 * cols), BF16)

        def arrived(e=e):
            edge_arrival(ITERS + 1, e).wait_recv()
            value = send[ITERS + 1, e] - recv[ITERS + 1, e] + dot(mbt[rows(e)], z_ref[...])
            u_ref[e] = value
            set_weights(e, value)

        pl.when(exists[e])(arrived)

    def edges_sent(t, which=range(4)):
        for e in which:
            pl.when(exists[e])(lambda e=e: edge_copy(t, e).wait_send())

    def sums_sent(k):
        @pl.when(j > 0)
        def _():
            bytes_of(first.at[k, pl.ds(0, 2 * nx - 1)], f_send.at[k]).wait()

        @pl.when(j == 0)
        def _():
            bytes_of(first.at[k, pl.ds(0, nx - 1)], f_send.at[k]).wait()

        bytes_of(second.at[k, pl.ds(0, ny - 1)], g_send.at[k]).wait()

    def step_along(beta, step):
        for n, e in enumerate((1, 3)):
            direction = u_ref[e] + beta * p_ref[n]
            p_ref[n] = direction
            mult_ref[n] = mult_ref[n] + step * direction

    def iteration(k, carry):
        t = ITERS + 1 + k
        open_iteration(k, False)
        second_stage(k)
        precondition_edges(k, t)
        rz, energy, beta, step = scalars_of(k, *carry)
        step_along(beta, step)
        update_residual(k, beta, step)
        for e in range(4):
            weights[rows(e)] = jnp.zeros((edge, 2 * cols), BF16)

            def arrived(e=e):
                edge_arrival(t, e).wait_recv()
                image = send[t, e] - recv[t, e] + dot(mbt[rows(e)], z_ref[...])
                image = image + beta * q_ref[e]
                q_ref[e] = image
                value = u_ref[e] - step * image
                u_ref[e] = value
                set_weights(e, value)

            pl.when(exists[e])(arrived)
        return rz, energy

    rz, energy = lax.fori_loop(1, ITERS, iteration, (one_row, zero_row))
    open_iteration(ITERS, True)
    second_stage(ITERS)
    rz, energy, beta, step = scalars_of(ITERS, rz, energy)
    step_along(beta, step)
    for n, e in enumerate((1, 3)):
        resid_ref[n] = jnp.zeros((edge, cols), F32)

        def arrived(n=n, e=e):
            edge_arrival(ITERS, e).wait_recv()
            image = send[ITERS, e] - recv[ITERS, e] + dot(bt[rows(e)], z_ref[...])
            resid_ref[n] = r_ref[e] - step * (image + beta * s_ref[e])

        pl.when(exists[e])(arrived)

    for e in range(4):

        def sent(e=e):
            couple_copy(e).wait_send()
            image_copy(e).wait_send()

        pl.when(exists[e])(sent)

    edges_sent(ITERS, (0, 2))

    @pl.loop(0, 2 * ITERS + 1)
    def _(t):
        pl.when(t != ITERS)(lambda: edges_sent(t))

    @pl.loop(0, ITERS + 1)
    def _(k):
        sums_sent(k)


def per_device(loads, flex, schur, couple, corner_perm, coarse_inverse):
    nx = lax.axis_size("sx")
    ny = lax.axis_size("sy")
    iface, cols = loads.shape[2:]
    edge = iface // 4
    nc = coarse_inverse.shape[0]
    ncp = -(-nc // 128) * 128
    group = -(-(nx - 1) // 8) * 8 + 8
    kdim = ny * group
    steps = 2 * ITERS + 1
    rounds = ITERS + 1
    vmem = pl.BlockSpec(memory_space=pltpu.VMEM)
    hbm = pl.BlockSpec(memory_space=pl.ANY)
    dma = pltpu.SemaphoreType.DMA
    out = jax.ShapeDtypeStruct((2, edge, cols), F32)
    mult, resid = pl.pallas_call(
        functools.partial(kernel, nx, ny, edge, group),
        out_shape=(out, out),
        in_specs=[hbm, hbm, hbm, hbm, vmem, hbm],
        out_specs=(vmem, vmem),
        scratch_shapes=[
            pltpu.VMEM((iface, cols), BF16),
            pltpu.VMEM((4, iface), F32),
            pltpu.VMEM((nc, nc), F32),
            pltpu.VMEM((iface, iface), F32),
            pltpu.VMEM((4, 2 * edge, iface), BF16),
            pltpu.VMEM((iface, iface), BF16),
            pltpu.VMEM((ncp, ncp), F32),
            pltpu.VMEM((2, kdim, kdim), BF16),
            pltpu.VMEM((2, ZROWS + 8, kdim), BF16),
            pltpu.VMEM((group, 2 * nx * 8), BF16),
            pltpu.VMEM((32, iface), BF16),
            pltpu.VMEM((4, 8, edge), F32),
            pltpu.VMEM((4, 8, edge), F32),
            pltpu.VMEM((ZROWS, iface), F32),
            pltpu.VMEM((iface, 3 * ZROWS), BF16),
            pltpu.VMEM((4, ZROWS, edge), F32),
            pltpu.VMEM((4, ZROWS, edge), F32),
            pltpu.VMEM((iface, 3 * ZROWS), BF16),
            pltpu.VMEM((steps, 4, edge, cols), F32),
            pltpu.VMEM((steps, 4, edge, cols), F32),
            pltpu.VMEM((rounds, 8, cols), F32),
            pltpu.VMEM((rounds, 8, cols), F32),
            pltpu.VMEM((rounds, 2 * nx, 8, cols), F32),
            pltpu.VMEM((rounds, group, cols), F32),
            pltpu.VMEM((rounds, ny, group, cols), F32),
            pltpu.VMEM((4, edge, cols), F32),
            pltpu.VMEM((iface, 2 * cols), BF16),
            pltpu.VMEM((3 * ZROWS, cols), BF16),
            pltpu.VMEM((4, edge, cols), F32),
            pltpu.VMEM((4, edge, cols), F32),
            pltpu.VMEM((4, edge, cols), F32),
            pltpu.VMEM((2, edge, cols), F32),
            dma((3,)),
            dma((4,)),
            dma,
            dma((4,)),
            dma((4,)),
            dma((4,)),
            dma((4,)),
            dma((steps, 4)),
            dma((steps, 4)),
            dma((rounds,)),
            dma((rounds,)),
            dma((rounds,)),
            dma((rounds,)),
        ],
        compiler_params=pltpu.CompilerParams(
            collective_id=0, has_side_effects=True, vmem_limit_bytes=60 * 1024 * 1024
        ),
    )(loads[0, 0], flex[0, 0], schur[0, 0], couple[0, 0], corner_perm.reshape(1, nc), coarse_inverse)
    return mult[None, None], resid[None, None]


def solution(mesh):
    placed = (
        P("sx", "sy", None, None),
        P("sx", "sy", None, None),
        P("sx", "sy", None, None),
        P("sx", "sy", None, None),
        P(),
        P(),
    )
    return jax.shard_map(
        per_device,
        mesh=mesh,
        in_specs=placed,
        out_specs=(P("sx", "sy", None, None, None), P("sx", "sy", None, None, None)),
        check_vma=False,
    )
```
